32 devices in a mesh: dp: 2 (over x), expert: 16 (over z, y, core).
Axes of the slice: x: 2, y: 2, z: 4, core: 2. Of those that a mesh axis runs over, the one named last changes fastest.
Arguments:
- tokens: bfloat16 [4096, 2048], P(('dp', 'expert')), may hold values from -6 to 6
- cotangent: bfloat16 [4096, 2048], P(('dp', 'expert')), may hold values from -0.875 to 0.875
- expert_ids: int32 [4096, 8], P(('dp', 'expert')), may hold values from 0 to 15, all different within a row; in each aligned block of 128 rows (0 to 127, 128 to 255, ...) at most 72 rows name the same one
- combine: float32 [4096, 8], P(('dp', 'expert')), may hold values from 0.02 to 0.5
- w_gate: bfloat16 [16, 2048, 512], P('expert'), may hold values from -0.125 to 0.125
- w_up: bfloat16 [16, 2048, 512], P('expert'), may hold values from -0.125 to 0.125
- w_down: bfloat16 [16, 512, 2048], P('expert'), may hold values from -0.25 to 0.25
- tangent_gate: bfloat16 [16, 2048, 512], P('expert'), may hold values from -0.125 to 0.125
Outputs:
- hvp_gate: float32 [16, 2048, 512], P('expert', 'dp')
- output_tangent: bfloat16 [4096, 2048], P(('dp', 'expert'))
The draws below stay inside these ranges and needn't reach their ends.
Inputs may be any that keep to these rules, and one draw needn't show every extreme that they name: `expert_ids`: A row names 8 different experts; among the 128 rows of one device no expert is named by more than 72 rows, and in every draw some expert is named by exactly 72 rows of some device.
All inputs are finite; a program needn't handle non-finite values.
Results may differ from the reference program's by a relative error of at most 0.0057.
Values may be sent and summed in bfloat16 or wider, within the bound.
A program may use at most 128 MiB of HBM per device.

```python
import math
import jax
import jax.numpy as jnp
import numpy as np
from jax import lax

D = 2048
FF = 512
TOPK = 8
TOK_DEV = 128
EXPERTS = 16
CAP = 72
TOKENS = 4096
N_DP = 2
N_EXPERT = 16


def steps_of(stream_key, shape, cuts, least, largest):
    def one(position, blocks):
        heights = jax.random.uniform(jax.random.fold_in(jax.random.fold_in(stream_key, 6), position), (blocks,), jnp.float32, least / len(cuts), largest / len(cuts))
        return jnp.repeat(jnp.exp(heights), shape[position] // blocks).reshape((-1,) + (1,) * (len(shape) - position - 1))

    level = one(*cuts[0])
    for cut in cuts[1:]:
        level = level * one(*cut)
    return level


def shared_out(key, own, number, rows, count, top, reach, slope):
    order = jax.random.permutation(key, count)
    packed, common = portions_of(count, rows * top, reach, slope, True), portions_of(count, rows * top, reach, slope, False)
    places = jnp.arange(count)

    def named(lengths, offset_by):
        used = int((lengths > 0).sum())
        fixed = max(1, used // 4)
        shifted = fixed + (places - fixed + offset_by * (used - fixed)) % max(1, count - fixed)
        return jnp.zeros((count,), jnp.int32).at[order[jnp.where(places < fixed, places, shifted)]].set(jnp.asarray(lengths, jnp.int32))

    lengths = jnp.where(number % 4 == 0, named(packed, number // 4), named(common, number - number // 4 - 1))
    mixed = jax.random.permutation(jax.random.fold_in(own, 3), count)
    source_of, receiver = mixed[0:count // 2 * 2:2], mixed[1:count // 2 * 2:2]
    slack = jnp.minimum(lengths[source_of] - 1, reach - lengths[receiver]) // 2
    slack = jnp.where((source_of == order[0]) | (receiver == order[0]) | (lengths[receiver] == 0), 0, jnp.maximum(slack, 0))
    shifted = jax.random.randint(jax.random.fold_in(own, 4), (count // 2,), 0, 1 << 20) % (slack + 1)
    lengths = lengths.at[source_of].add(-shifted).at[receiver].add(shifted)
    members = jnp.searchsorted(jnp.cumsum(lengths), jnp.arange(rows * top), side="right").astype(jnp.int32)
    grid = members.reshape(top, rows).T
    grid = grid[jax.random.permutation(jax.random.fold_in(own, 1), rows)]
    offset_by = jax.random.randint(jax.random.fold_in(own, 2), (rows, 1), 0, top)
    return jnp.take_along_axis(grid, (jnp.arange(top)[None, :] + offset_by) % top, axis=1)


def portions_of(number_of, total, limit, lean, full):
    weights = [(1 << 20) // math.isqrt(standing ** lean) + 1 for standing in range(1, number_of + 1)]
    largest = limit if full else min(limit, max(-(-total // number_of), total * weights[0] // sum(weights)))
    least = 1 if total - largest >= number_of - 1 else 0
    holding, spare = [largest] + [least] * (number_of - 1), total - largest - least * (number_of - 1)
    while spare > 0:
        free = [i for i in range(1, number_of) if holding[i] < largest] or [i for i in range(1, number_of) if holding[i] < limit]
        whole, remaining = sum([weights[i] for i in free]), spare
        for i in free:
            addition = min(limit - holding[i], max(1, remaining * weights[i] // whole), spare)
            holding[i] = holding[i] + addition
            spare = spare - addition
    return np.array(holding)


def noise(stream_key, dims, deviation, reach, shards=(), held_as=jnp.bfloat16):
    drawn = jax.random.normal(stream_key, dims, jnp.float32) * deviation
    if len(shards) > 0:
        drawn = steps_of(stream_key, dims, shards, -0.22, 0.18) * drawn
    return jnp.clip(drawn, min=-reach, max=reach).astype(held_as)


def setup_inputs(seed: int = 0) -> dict:
    key_of = jax.random.split(jax.random.key(seed), 9)
    tokens = noise(key_of[0], (TOKENS, D), 1.0, 6.0, ((0, 32),))
    cotangent = noise(key_of[1], (TOKENS, D), 0.15, 0.875, ((0, 32),))
    expert_ids_keys = jax.random.split(jax.random.fold_in(key_of[2], 1), TOKENS // TOK_DEV)
    expert_ids_turns = jax.random.permutation(jax.random.fold_in(key_of[2], 3), TOKENS // TOK_DEV)
    expert_ids = jax.vmap(lambda own, number: shared_out(jax.random.fold_in(key_of[2], 2), own, number, TOK_DEV, EXPERTS, TOPK, CAP, 1))(expert_ids_keys, expert_ids_turns).reshape((TOKENS, TOPK))
    combine = jnp.clip(jnp.exp(math.log(0.5) - 3.218876 * jax.random.uniform(key_of[3], (TOKENS, TOPK), jnp.float32) ** steps_of(key_of[3], (TOKENS, TOPK), ((0, 32),), -0.2, 0.2)), 0.02, 0.5)
    w_gate = noise(key_of[4], (EXPERTS, D, FF), D ** -0.5, 0.125, ((0, 16),))
    w_up = noise(key_of[5], (EXPERTS, D, FF), D ** -0.5, 0.125, ((0, 16),))
    w_down = noise(key_of[6], (EXPERTS, FF, D), FF ** -0.5, 0.25, ((0, 16),))
    tangent_gate = noise(key_of[7], (EXPERTS, D, FF), D ** -0.5, 0.125, ((0, 16),))
    return {"tokens": tokens, "cotangent": cotangent, "expert_ids": expert_ids, "combine": combine, "w_gate": w_gate, "w_up": w_up, "w_down": w_down, "tangent_gate": tangent_gate}


def silu_derivs(gate_act):
    squash = jax.nn.sigmoid(gate_act)
    first = squash * (1.0 + gate_act * (1.0 - squash))
    second = squash * (1.0 - squash) * (2.0 + gate_act * (1.0 - 2.0 * squash))
    return first, second


def expert_rows(rows, scaled, gate_e, up_e, down_e, tangent_e):
    gate_act = jnp.dot(rows, gate_e, preferred_element_type=jnp.float32)
    up_act = jnp.dot(rows, up_e, preferred_element_type=jnp.float32)
    gate_dot = jnp.dot(rows, tangent_e, preferred_element_type=jnp.float32)
    first, second = silu_derivs(gate_act)
    lifted = (first * gate_dot * up_act).astype(jnp.bfloat16)
    term = jnp.dot(lifted, down_e, preferred_element_type=jnp.float32).astype(jnp.bfloat16)
    factor = up_act * second * gate_dot
    back_hidden = lax.dot_general(scaled, down_e, (((1,), (1,)), ((), ())), preferred_element_type=jnp.float32)
    coeff = (back_hidden * factor).astype(jnp.bfloat16)
    partial_hvp = lax.dot_general(rows, coeff, (((0,), (0,)), ((), ())), preferred_element_type=jnp.float32)
    return term, partial_hvp


def reference(tokens, cotangent, expert_ids, combine, w_gate, w_up, w_down, tangent_gate):
    max_rows = N_DP * N_EXPERT * CAP
    token_count = tokens.shape[0]

    def visit(accumulate, stacked):
        expert_index, gate_e, up_e, down_e, tangent_e = stacked
        chosen = expert_ids == expert_index
        present = jnp.any(chosen, axis=1)
        weight_all = jnp.sum(jnp.where(chosen, combine, jnp.zeros_like(combine)), axis=1)
        row_index = jnp.nonzero(present, size=max_rows, fill_value=0)[0].astype(jnp.int32)
        valid = jnp.arange(max_rows, dtype=jnp.int32) < jnp.sum(present.astype(jnp.int32))
        picked_weight = weight_all[row_index]
        row_weight = jnp.where(valid, picked_weight, jnp.zeros_like(picked_weight))
        rows = tokens[row_index]
        scaled = (row_weight[:, None] * cotangent[row_index].astype(jnp.float32)).astype(jnp.bfloat16)
        term, partial_hvp = expert_rows(rows, scaled, gate_e, up_e, down_e, tangent_e)
        accumulate = accumulate.at[row_index].add(row_weight[:, None] * term.astype(jnp.float32))
        return accumulate, partial_hvp

    start_value = jnp.zeros((token_count, tokens.shape[1]), jnp.float32)
    numbers = jnp.arange(EXPERTS, dtype=jnp.int32)
    final, hvp_gate = lax.scan(visit, start_value, (numbers, w_gate, w_up, w_down, tangent_gate))
    return hvp_gate, final.astype(jnp.bfloat16)
```

```python
import jax
import jax.numpy as jnp
from jax import lax
from jax.sharding import PartitionSpec as P


def silu_derivs(gate_act):
    squash = jax.nn.sigmoid(gate_act)
    first = squash * (1.0 + gate_act * (1.0 - squash))
    second = squash * (1.0 - squash) * (2.0 + gate_act * (1.0 - 2.0 * squash))
    return (first, second)


def weight_table(expert_ids, combine, expert_count):
    owners = jnp.arange(expert_count, dtype=jnp.int32)
    chosen = expert_ids[:, :, None] == owners[None, None, :]
    return jnp.sum(jnp.where(chosen, combine[:, :, None], 0.0), axis=1).T


def per_device(tokens, cotangent, expert_ids, combine, w_gate, w_up, w_down, tangent_gate):
    expert_count = lax.axis_size("expert")
    rows_dev, top_count = expert_ids.shape
    model_width = tokens.shape[1]
    capacity = rows_dev * top_count * 9 // (8 * expert_count)
    table = weight_table(expert_ids, combine, expert_count)
    weights = lax.all_to_all(table, "expert", split_axis=0, concat_axis=0, tiled=True)
    tokens_all = lax.all_gather(tokens, "expert", axis=0)
    cotangent_all = lax.all_gather(cotangent, "expert", axis=0)
    present = weights > 0.0
    counted = present.astype(jnp.int32)
    position = jnp.cumsum(counted, axis=1) - counted
    slots = jnp.arange(capacity, dtype=jnp.int32)
    hit = (position[:, None, :] == slots[None, :, None]) & present[:, None, :]
    select = hit.astype(jnp.bfloat16)
    slot_weight = jnp.sum(jnp.where(hit, weights[:, None, :], 0.0), axis=2).reshape(-1, 1)

    def pick(block):
        out = jnp.einsum("scr,srd->scd", select, block, preferred_element_type=jnp.float32)
        return out.reshape(-1, model_width)

    rows_flat = pick(tokens_all).astype(jnp.bfloat16)
    gate_act = jnp.dot(rows_flat, w_gate[0], preferred_element_type=jnp.float32)
    up_act = jnp.dot(rows_flat, w_up[0], preferred_element_type=jnp.float32)
    gate_dot = jnp.dot(rows_flat, tangent_gate[0], preferred_element_type=jnp.float32)
    first, second = silu_derivs(gate_act)
    lifted = (first * gate_dot * up_act).astype(jnp.bfloat16)
    term = jnp.dot(lifted, w_down[0], preferred_element_type=jnp.float32)
    weighted = (slot_weight * term).astype(jnp.bfloat16).reshape(expert_count, capacity, model_width)
    partial = jnp.einsum("scr,scd->srd", select, weighted, preferred_element_type=jnp.float32)
    partial = partial.astype(jnp.bfloat16).reshape(-1, model_width)
    output_tangent = lax.psum_scatter(partial, "expert", scatter_dimension=0, tiled=True)
    scaled = (slot_weight * pick(cotangent_all)).astype(jnp.bfloat16)
    back_hidden = lax.dot_general(
        scaled, w_down[0], (((1,), (1,)), ((), ())), preferred_element_type=jnp.float32
    )
    coeff = (back_hidden * (up_act * second * gate_dot)).astype(jnp.bfloat16)
    partial_hvp = lax.dot_general(
        rows_flat, coeff, (((0,), (0,)), ((), ())), preferred_element_type=jnp.float32
    )
    hvp_gate = lax.psum_scatter(partial_hvp, "dp", scatter_dimension=0, tiled=True)
    return (hvp_gate[None], output_tangent)


def solution(mesh):
    rows = P(("dp", "expert"), None)
    owned = P("expert", None, None)
    return jax.shard_map(
        per_device,
        mesh=mesh,
        in_specs=(rows, rows, rows, rows, owned, owned, owned, owned),
        out_specs=(P("expert", "dp", None), rows),
        check_vma=False,
    )
```

```python
import functools
import jax
import jax.numpy as jnp
from jax import lax
from jax.experimental import pallas as pl
from jax.experimental.pallas import tpu as pltpu
from jax.sharding import PartitionSpec as P


def silu_derivs(gate_act):
    squash = jax.nn.sigmoid(gate_act)
    first = squash * (1.0 + gate_act * (1.0 - squash))
    second = squash * (1.0 - squash) * (2.0 + gate_act * (1.0 - 2.0 * squash))
    return (first, second)


def weight_table(expert_ids, combine, expert_count):
    owners = jnp.arange(expert_count, dtype=jnp.int32)
    chosen = expert_ids[:, :, None] == owners[None, None, :]
    return jnp.sum(jnp.where(chosen, combine[:, :, None], 0.0), axis=1).T


def gathered(tokens, cotangent, expert_ids, combine, w_gate, w_up, w_down, tangent_gate):
    expert_count = lax.axis_size("expert")
    rows_dev, top_count = expert_ids.shape
    model_width = tokens.shape[1]
    capacity = rows_dev * top_count * 9 // (8 * expert_count)
    table = weight_table(expert_ids, combine, expert_count)
    weights = lax.all_to_all(table, "expert", split_axis=0, concat_axis=0, tiled=True)
    tokens_all = lax.all_gather(tokens, "expert", axis=0)
    cotangent_all = lax.all_gather(cotangent, "expert", axis=0)
    present = weights > 0.0
    counted = present.astype(jnp.int32)
    position = jnp.cumsum(counted, axis=1) - counted
    slots = jnp.arange(capacity, dtype=jnp.int32)
    hit = (position[:, None, :] == slots[None, :, None]) & present[:, None, :]
    select = hit.astype(jnp.bfloat16)
    slot_weight = jnp.sum(jnp.where(hit, weights[:, None, :], 0.0), axis=2).reshape(-1, 1)

    def pick(block):
        out = jnp.einsum("scr,srd->scd", select, block, preferred_element_type=jnp.float32)
        return out.reshape(-1, model_width)

    rows_flat = pick(tokens_all).astype(jnp.bfloat16)
    gate_act = jnp.dot(rows_flat, w_gate[0], preferred_element_type=jnp.float32)
    up_act = jnp.dot(rows_flat, w_up[0], preferred_element_type=jnp.float32)
    gate_dot = jnp.dot(rows_flat, tangent_gate[0], preferred_element_type=jnp.float32)
    first, second = silu_derivs(gate_act)
    lifted = (first * gate_dot * up_act).astype(jnp.bfloat16)
    term = jnp.dot(lifted, w_down[0], preferred_element_type=jnp.float32)
    weighted = (slot_weight * term).astype(jnp.bfloat16).reshape(expert_count, capacity, model_width)
    partial = jnp.einsum("scr,scd->srd", select, weighted, preferred_element_type=jnp.float32)
    partial = partial.astype(jnp.bfloat16).reshape(-1, model_width)
    output_tangent = lax.psum_scatter(partial, "expert", scatter_dimension=0, tiled=True)
    scaled = (slot_weight * pick(cotangent_all)).astype(jnp.bfloat16)
    back_hidden = lax.dot_general(
        scaled, w_down[0], (((1,), (1,)), ((), ())), preferred_element_type=jnp.float32
    )
    coeff = (back_hidden * (up_act * second * gate_dot)).astype(jnp.bfloat16)
    partial_hvp = lax.dot_general(
        rows_flat, coeff, (((0,), (0,)), ((), ())), preferred_element_type=jnp.float32
    )
    hvp_gate = lax.psum_scatter(partial_hvp, "dp", scatter_dimension=0, tiled=True)
    return (hvp_gate[None], output_tangent)


NZ, NY, NC = 4, 2, 2


def kernel(
    capacity,
    table_ref, tokens_ref, cot_ref, gate_ref, up_ref, down_ref, tan_ref,
    hvp_ref, out_ref,
    table, tok, cot, rows, factor, coeff, part, sib_in, y_in, z_in, x_out, x_in,
    g_send, g_recv, s_send, s_recv, y_send, y_recv, z_send, z_recv, x_send, x_recv,
):
    f32, b16 = jnp.float32, jnp.bfloat16
    dp, me = lax.axis_index("dp"), lax.axis_index("expert")
    c, y, z = me % NC, (me // NC) % NY, me // (NC * NY)
    n = tokens_ref.shape[0]
    pairs = NZ * NY
    height = NC * capacity
    half = hvp_ref.shape[0]

    def at(zz, yy, cc):
        return (zz * NY + yy) * NC + cc

    def zj(j):
        return (z + j) % NZ

    def yj(j):
        return (y + j // NZ) % NY

    sibling, across = at(z, y, 1 - c), at(z, 1 - y, c)
    other = (1 - dp, me)
    peers = [(dp, sibling), (dp, across), other] + [(dp, at(zj(j), y, c)) for j in range(1, NZ)]
    barrier = pltpu.get_barrier_semaphore()
    for peer in peers:
        pl.semaphore_signal(barrier, inc=1, device_id=peer, device_id_type=pl.DeviceIdType.MESH)
    pl.semaphore_wait(barrier, len(peers))

    def remote(src, dst, send, recv, peer):
        return pltpu.make_async_remote_copy(
            src_ref=src, dst_ref=dst, send_sem=send, recv_sem=recv,
            device_id=peer, device_id_type=pl.DeviceIdType.MESH,
        )

    sent = []

    def begin(copy):
        copy.start()
        sent.append(copy)

    fulls = (table, tok, cot)
    owns = (table_ref, tokens_ref, cot_ref)

    def piece(a, b):
        return table.at[b] if a == 0 else fulls[a].at[pl.ds(b * n, n)]

    def send_block(a, src, b, slot, peer):
        begin(remote(src, piece(a, b), g_send.at[a, slot], g_recv.at[a, b], peer))

    def arrived(a, b):
        remote(piece(a, b), piece(a, b), g_send.at[a, 0], g_recv.at[a, b], (dp, sibling)).wait_recv()

    def send_own(a):
        send_block(a, owns[a], me, 0, (dp, across))
        for j in range(1, NZ):
            send_block(a, owns[a], me, j, (dp, at(zj(j), y, c)))
        send_block(a, owns[a], me, NZ, (dp, sibling))

    def pass_row(a, j):
        b = at(zj(j), y, c)
        arrived(a, b)
        send_block(a, piece(a, b), b, NZ + j, (dp, across))
        send_block(a, piece(a, b), b, 2 * NZ - 1 + j, (dp, sibling))

    def pass_across(a, j):
        b = at(zj(j), 1 - y, c)
        arrived(a, b)
        send_block(a, piece(a, b), b, 3 * NZ - 1 + j, (dp, sibling))

    send_own(0)
    send_own(1)
    table[me] = table_ref[...]
    tok[pl.ds(me * n, n), :] = tokens_ref[...]
    cot[pl.ds(me * n, n), :] = cot_ref[...]
    for j in range(1, NZ):
        pass_row(0, j)
        pass_row(1, j)
    send_own(2)

    def choose(j):
        base = at(zj(j), yj(j), 0)
        owner = lax.broadcasted_iota(jnp.int32, (table.shape[1], n), 0) == me
        earlier = lax.broadcasted_iota(jnp.int32, (n, n), 0) < lax.broadcasted_iota(
            jnp.int32, (n, n), 1
        )
        earlier = earlier.astype(f32).astype(b16)
        weights, places = [], []
        for cc in range(NC):
            w = jnp.sum(jnp.where(owner, table[base + cc], 0.0), axis=0, keepdims=True)
            present = jnp.where(jnp.broadcast_to(w, (16, n)) > 0.0, 1.0, 0.0).astype(b16)
            place = jnp.dot(present, earlier, preferred_element_type=f32)[0:1, :]
            weights.append(w)
            places.append(place + float(cc * capacity))
        w, place = jnp.concatenate(weights, axis=1), jnp.concatenate(places, axis=1)
        slot = lax.broadcasted_iota(jnp.int32, (height, NC * n), 0).astype(f32)
        hit = (slot == place) & (w > 0.0)
        select = jnp.where(hit, 1.0, 0.0)
        slot_weight = jnp.sum(jnp.where(hit, w, 0.0), axis=1, keepdims=True)
        return base, select.astype(b16), slot_weight

    def forward(j0):
        found = []
        for k in range(2):
            base, select, slot_weight = choose(j0 + k)
            both = tok[pl.ds(base * n, NC * n), :]
            mine = jnp.dot(select, both, preferred_element_type=f32).astype(b16)
            rows[pl.ds((j0 + k) * height, height), :] = mine
            found.append((select, slot_weight))
        at_rows = pl.ds(j0 * height, 2 * height)
        held = rows[at_rows, :]
        gate_act = jnp.dot(held, gate_ref[...], preferred_element_type=f32)
        up_act = jnp.dot(held, up_ref[...], preferred_element_type=f32)
        gate_dot = jnp.dot(held, tan_ref[...], preferred_element_type=f32)
        first, second = silu_derivs(gate_act)
        factor[at_rows, :] = up_act * second * gate_dot
        lifted = first * gate_dot * up_act
        for k in range(2):
            select, slot_weight = found[k]
            one = (lifted[k * height:(k + 1) * height] * slot_weight).astype(b16)
            spread = lax.dot_general(
                select, one, (((0,), (0,)), ((), ())), preferred_element_type=f32
            ).astype(b16)
            part[j0 + k] = jnp.dot(spread, down_ref[...], preferred_element_type=f32).astype(b16)

    def from_sibling(a, j0):
        for k in range(2):
            arrived(a, at(zj(j0 + k), yj(j0 + k), 1 - c))

    def to_sibling(j):
        begin(remote(
            part.at[j, pl.ds((1 - c) * n, n)], sib_in.at[j], s_send.at[j], s_recv.at[j],
            (dp, sibling),
        ))

    def landed(buf, sem):
        remote(buf, buf, s_send.at[0], sem, (dp, sibling)).wait_recv()

    def group(j0):
        from_sibling(0, j0)
        from_sibling(1, j0)
        forward(j0)
        to_sibling(j0)
        to_sibling(j0 + 1)

    group(0)
    group(2)
    for j in range(NZ):
        pass_across(0, j)
        pass_across(1, j)
    for j in range(1, NZ):
        pass_row(2, j)
    group(4)
    group(6)

    def own_half(j):
        return part.at[j, pl.ds(c * n, n)]

    def chip_sum(j):
        landed(sib_in.at[j], s_recv.at[j])
        return own_half(j)[...].astype(f32) + sib_in[j].astype(f32)

    for j in (5, 6, 7, 4):
        own_half(j)[...] = chip_sum(j).astype(b16)
        begin(remote(own_half(j), y_in.at[j - NZ], y_send.at[j - NZ], y_recv.at[j - NZ], (dp, across)))
    for j in range(NZ):
        pass_across(2, j)

    for j0 in range(0, pairs, 2):
        from_sibling(2, j0)
        for k in range(2):
            base, select, slot_weight = choose(j0 + k)
            both = cot[pl.ds(base * n, NC * n), :]
            scaled = (slot_weight * jnp.dot(select, both, preferred_element_type=f32)).astype(b16)
            back = lax.dot_general(
                scaled, down_ref[...], (((1,), (1,)), ((), ())), preferred_element_type=f32
            )
            at_rows = pl.ds((j0 + k) * height, height)
            coeff[at_rows, :] = (back * factor[at_rows, :]).astype(b16)

    wide = half // 4

    def product(start):
        cols = rows[:, pl.ds(pl.multiple_of(start, 128), wide)]
        return lax.dot_general(
            cols, coeff[...], (((0,), (0,)), ((), ())), preferred_element_type=f32
        )

    for q in range(4):
        some = pl.ds(q * wide, wide)
        x_out[some, :] = product((1 - dp) * half + q * wide).astype(b16)
        begin(remote(x_out.at[some], x_in.at[some], x_send.at[q], x_recv.at[q], other))

    for j in (1, 2, 3, 0):
        total = chip_sum(j)
        landed(y_in.at[j], y_recv.at[j])
        total = total + y_in[j].astype(f32)
        own_half(j)[...] = total.astype(b16)
        if j > 0:
            begin(remote(
                own_half(j), z_in.at[j - 1], z_send.at[j - 1], z_recv.at[j - 1],
                (dp, at(zj(j), y, c)),
            ))
    for q in range(4):
        hvp_ref[pl.ds(q * wide, wide), :] = product(dp * half + q * wide)
    for q in range(4):
        some = pl.ds(q * wide, wide)
        landed(x_in.at[some], x_recv.at[q])
        hvp_ref[some, :] = hvp_ref[some, :] + x_in[some, :].astype(f32)
    for j in range(NZ - 1):
        landed(z_in.at[j], z_recv.at[j])
    out_ref[...] = (
        own_half(0)[...].astype(f32) + z_in[0].astype(f32)
        + z_in[1].astype(f32) + z_in[2].astype(f32)
    ).astype(b16)
    for copy in sent:
        copy.wait_send()


def fused(tokens, cotangent, expert_ids, combine, w_gate, w_up, w_down, tangent_gate):
    count = lax.axis_size("expert")
    n, top = expert_ids.shape
    width, hidden = w_gate.shape[1:]
    capacity = n * top * 9 // (8 * count)
    total = count * capacity
    b16, f32 = jnp.bfloat16, jnp.float32
    dma = pltpu.SemaphoreType.DMA
    pairs = NZ * NY
    whole = pl.BlockSpec(memory_space=pltpu.VMEM)
    hvp, out = pl.pallas_call(
        functools.partial(kernel, capacity),
        out_shape=(
            jax.ShapeDtypeStruct((width // 2, hidden), f32),
            jax.ShapeDtypeStruct((n, width), b16),
        ),
        in_specs=[whole] * 7,
        out_specs=(whole, whole),
        scratch_shapes=[
            pltpu.VMEM((count, count, n), f32),
            pltpu.VMEM((count * n, width), b16),
            pltpu.VMEM((count * n, width), b16),
            pltpu.VMEM((total, width), b16),
            pltpu.VMEM((total, hidden), f32),
            pltpu.VMEM((total, hidden), b16),
            pltpu.VMEM((pairs, NC * n, width), b16),
            pltpu.VMEM((pairs, n, width), b16),
            pltpu.VMEM((NZ, n, width), b16),
            pltpu.VMEM((NZ - 1, n, width), b16),
            pltpu.VMEM((width // 2, hidden), b16),
            pltpu.VMEM((width // 2, hidden), b16),
            dma((3, 4 * NZ - 1)), dma((3, count)),
            dma((pairs,)), dma((pairs,)),
            dma((NZ,)), dma((NZ,)),
            dma((NZ - 1,)), dma((NZ - 1,)),
            dma((4,)), dma((4,)),
        ],
        compiler_params=pltpu.CompilerParams(
            collective_id=0, has_side_effects=True, vmem_limit_bytes=63 * 1024 * 1024
        ),
    )(
        weight_table(expert_ids, combine, count), tokens, cotangent,
        w_gate[0], w_up[0], w_down[0], tangent_gate[0],
    )
    return hvp[None], out


def per_device(*arrays):
    if lax.axis_size("expert") == NZ * NY * NC and lax.axis_size("dp") == 2:
        return fused(*arrays)
    return gathered(*arrays)


def solution(mesh):
    rows = P(("dp", "expert"), None)
    owned = P("expert", None, None)
    return jax.shard_map(
        per_device,
        mesh=mesh,
        in_specs=(rows, rows, rows, rows, owned, owned, owned, owned),
        out_specs=(P("expert", "dp", None), rows),
        check_vma=False,
    )
```

```python
import functools
import jax
import jax.numpy as jnp
from jax import lax
from jax.experimental import pallas as pl
from jax.experimental.pallas import tpu as pltpu
from jax.sharding import PartitionSpec as P


def silu_derivs(gate_act):
    squash = jax.nn.sigmoid(gate_act)
    first = squash * (1.0 + gate_act * (1.0 - squash))
    second = squash * (1.0 - squash) * (2.0 + gate_act * (1.0 - 2.0 * squash))
    return (first, second)


def weight_table(expert_ids, combine, expert_count):
    owners = jnp.arange(expert_count, dtype=jnp.int32)
    chosen = expert_ids[:, :, None] == owners[None, None, :]
    return jnp.sum(jnp.where(chosen, combine[:, :, None], 0.0), axis=1).T


def gathered(tokens, cotangent, expert_ids, combine, w_gate, w_up, w_down, tangent_gate):
    expert_count = lax.axis_size("expert")
    rows_dev, top_count = expert_ids.shape
    model_width = tokens.shape[1]
    capacity = rows_dev * top_count * 9 // (8 * expert_count)
    table = weight_table(expert_ids, combine, expert_count)
    weights = lax.all_to_all(table, "expert", split_axis=0, concat_axis=0, tiled=True)
    tokens_all = lax.all_gather(tokens, "expert", axis=0)
    cotangent_all = lax.all_gather(cotangent, "expert", axis=0)
    present = weights > 0.0
    counted = present.astype(jnp.int32)
    position = jnp.cumsum(counted, axis=1) - counted
    slots = jnp.arange(capacity, dtype=jnp.int32)
    hit = (position[:, None, :] == slots[None, :, None]) & present[:, None, :]
    select = hit.astype(jnp.bfloat16)
    slot_weight = jnp.sum(jnp.where(hit, weights[:, None, :], 0.0), axis=2).reshape(-1, 1)

    def pick(block):
        out = jnp.einsum("scr,srd->scd", select, block, preferred_element_type=jnp.float32)
        return out.reshape(-1, model_width)

    rows_flat = pick(tokens_all).astype(jnp.bfloat16)
    gate_act = jnp.dot(rows_flat, w_gate[0], preferred_element_type=jnp.float32)
    up_act = jnp.dot(rows_flat, w_up[0], preferred_element_type=jnp.float32)
    gate_dot = jnp.dot(rows_flat, tangent_gate[0], preferred_element_type=jnp.float32)
    first, second = silu_derivs(gate_act)
    lifted = (first * gate_dot * up_act).astype(jnp.bfloat16)
    term = jnp.dot(lifted, w_down[0], preferred_element_type=jnp.float32)
    weighted = (slot_weight * term).astype(jnp.bfloat16).reshape(expert_count, capacity, model_width)
    partial = jnp.einsum("scr,scd->srd", select, weighted, preferred_element_type=jnp.float32)
    partial = partial.astype(jnp.bfloat16).reshape(-1, model_width)
    output_tangent = lax.psum_scatter(partial, "expert", scatter_dimension=0, tiled=True)
    scaled = (slot_weight * pick(cotangent_all)).astype(jnp.bfloat16)
    back_hidden = lax.dot_general(
        scaled, w_down[0], (((1,), (1,)), ((), ())), preferred_element_type=jnp.float32
    )
    coeff = (back_hidden * (up_act * second * gate_dot)).astype(jnp.bfloat16)
    partial_hvp = lax.dot_general(
        rows_flat, coeff, (((0,), (0,)), ((), ())), preferred_element_type=jnp.float32
    )
    hvp_gate = lax.psum_scatter(partial_hvp, "dp", scatter_dimension=0, tiled=True)
    return (hvp_gate[None], output_tangent)


NZ, NY, NC = 4, 2, 2


def kernel(
    capacity,
    table_ref, tokens_ref, cot_ref, gate_ref, up_ref, down_ref, tan_ref,
    hvp_ref, out_ref,
    table, tok, cot, rows, factor, coeff, part, sib_in, y_in, z_in, x_out, x_in,
    g_send, g_recv, s_send, s_recv, y_send, y_recv, z_send, z_recv, x_send, x_recv,
):
    f32, b16 = jnp.float32, jnp.bfloat16
    dp, me = lax.axis_index("dp"), lax.axis_index("expert")
    c, y, z = me % NC, (me // NC) % NY, me // (NC * NY)
    n = tokens_ref.shape[0]
    pairs = NZ * NY
    height = NC * capacity
    half = hvp_ref.shape[0]

    def at(zz, yy, cc):
        return (zz * NY + yy) * NC + cc

    def zj(j):
        return (z + j) % NZ

    def yj(j):
        return (y + j // NZ) % NY

    sibling, across = at(z, y, 1 - c), at(z, 1 - y, c)
    other = (1 - dp, me)
    peers = [(dp, sibling), (dp, across), other] + [(dp, at(zj(j), y, c)) for j in range(1, NZ)]
    barrier = pltpu.get_barrier_semaphore()
    for peer in peers:
        pl.semaphore_signal(barrier, inc=1, device_id=peer, device_id_type=pl.DeviceIdType.MESH)
    pl.semaphore_wait(barrier, len(peers))

    def remote(src, dst, send, recv, peer):
        return pltpu.make_async_remote_copy(
            src_ref=src, dst_ref=dst, send_sem=send, recv_sem=recv,
            device_id=peer, device_id_type=pl.DeviceIdType.MESH,
        )

    sent = []

    def begin(copy):
        copy.start()
        sent.append((None, lambda: copy))

    def begin_if(test, make):
        @pl.when(test)
        def _():
            make().start()

        sent.append((test, make))

    fulls = (table, tok, cot)
    owns = (table_ref, tokens_ref, cot_ref)

    def piece(a, b):
        return table.at[b] if a == 0 else fulls[a].at[pl.ds(b * n, n)]

    def send_block(a, src, b, slot, peer):
        begin(remote(src, piece(a, b), g_send.at[a, slot], g_recv.at[a, b], peer))

    def arrived(a, b):
        remote(piece(a, b), piece(a, b), g_send.at[a, 0], g_recv.at[a, b], (dp, sibling)).wait_recv()

    def block_copy(a, src, b, slot, peer):
        return lambda: remote(src(), piece(a, b), g_send.at[a, slot], g_recv.at[a, b], peer)

    def send_own(a):
        send_block(a, owns[a], me, 0, (dp, across))
        for slot, step in ((2, -1), (3, 1)):
            near = z + step
            begin_if(
                (near >= 0) & (near < NZ),
                block_copy(a, lambda: owns[a], me, slot, (dp, at(near, y, c))),
            )
        send_block(a, owns[a], me, 1, (dp, sibling))

    def pass_row(a, d):
        for side, step in enumerate((-1, 1)):
            origin, onward = z + step * d, z - step
            b = at(origin, y, c)
            there = (origin >= 0) & (origin < NZ)

            @pl.when(there)
            def _():
                arrived(a, b)

            slot = 4 + (side * (NZ - 1) + d - 1) * 3
            source = lambda a=a, b=b: piece(a, b)
            begin_if(
                there & (onward >= 0) & (onward < NZ),
                block_copy(a, source, b, slot, (dp, at(onward, y, c))),
            )
            begin_if(there, block_copy(a, source, b, slot + 1, (dp, across)))
            begin_if(there, block_copy(a, source, b, slot + 2, (dp, sibling)))

    def pass_across(a, j):
        b = at(zj(j), 1 - y, c)
        arrived(a, b)
        send_block(a, piece(a, b), b, 6 * NZ - 2 + j, (dp, sibling))

    send_own(0)
    send_own(1)
    table[me] = table_ref[...]
    tok[pl.ds(me * n, n), :] = tokens_ref[...]
    cot[pl.ds(me * n, n), :] = cot_ref[...]
    for j in range(1, NZ):
        pass_row(0, j)
        pass_row(1, j)
    send_own(2)

    def choose(j):
        base = at(zj(j), yj(j), 0)
        owner = lax.broadcasted_iota(jnp.int32, (table.shape[1], n), 0) == me
        earlier = lax.broadcasted_iota(jnp.int32, (n, n), 0) < lax.broadcasted_iota(
            jnp.int32, (n, n), 1
        )
        earlier = earlier.astype(f32).astype(b16)
        weights, places = [], []
        for cc in range(NC):
            w = jnp.sum(jnp.where(owner, table[base + cc], 0.0), axis=0, keepdims=True)
            present = jnp.where(jnp.broadcast_to(w, (16, n)) > 0.0, 1.0, 0.0).astype(b16)
            place = jnp.dot(present, earlier, preferred_element_type=f32)[0:1, :]
            weights.append(w)
            places.append(place + float(cc * capacity))
        w, place = jnp.concatenate(weights, axis=1), jnp.concatenate(places, axis=1)
        slot = lax.broadcasted_iota(jnp.int32, (height, NC * n), 0).astype(f32)
        hit = (slot == place) & (w > 0.0)
        select = jnp.where(hit, 1.0, 0.0)
        slot_weight = jnp.sum(jnp.where(hit, w, 0.0), axis=1, keepdims=True)
        return base, select.astype(b16), slot_weight

    def forward(j0):
        found = []
        for k in range(2):
            base, select, slot_weight = choose(j0 + k)
            both = tok[pl.ds(base * n, NC * n), :]
            mine = jnp.dot(select, both, preferred_element_type=f32).astype(b16)
            rows[pl.ds((j0 + k) * height, height), :] = mine
            found.append((select, slot_weight))
        at_rows = pl.ds(j0 * height, 2 * height)
        held = rows[at_rows, :]
        gate_act = jnp.dot(held, gate_ref[...], preferred_element_type=f32)
        up_act = jnp.dot(held, up_ref[...], preferred_element_type=f32)
        gate_dot = jnp.dot(held, tan_ref[...], preferred_element_type=f32)
        first, second = silu_derivs(gate_act)
        factor[at_rows, :] = up_act * second * gate_dot
        lifted = first * gate_dot * up_act
        for k in range(2):
            select, slot_weight = found[k]
            one = (lifted[k * height:(k + 1) * height] * slot_weight).astype(b16)
            spread = lax.dot_general(
                select, one, (((0,), (0,)), ((), ())), preferred_element_type=f32
            ).astype(b16)
            part[j0 + k] = jnp.dot(spread, down_ref[...], preferred_element_type=f32).astype(b16)

    def from_sibling(a, j0):
        for k in range(2):
            arrived(a, at(zj(j0 + k), yj(j0 + k), 1 - c))

    def to_sibling(j):
        begin(remote(
            part.at[j, pl.ds((1 - c) * n, n)], sib_in.at[j], s_send.at[j], s_recv.at[j],
            (dp, sibling),
        ))

    def landed(buf, sem):
        remote(buf, buf, s_send.at[0], sem, (dp, sibling)).wait_recv()

    def group(j0):
        from_sibling(0, j0)
        from_sibling(1, j0)
        forward(j0)
        to_sibling(j0)
        to_sibling(j0 + 1)

    group(0)
    pass_row(2, 1)
    group(2)
    pass_row(2, 2)
    for j in range(NZ):
        pass_across(0, j)
        pass_across(1, j)
    pass_row(2, 3)
    group(4)
    group(6)

    def own_half(j):
        return part.at[j, pl.ds(c * n, n)]

    def chip_sum(j):
        landed(sib_in.at[j], s_recv.at[j])
        return own_half(j)[...].astype(f32) + sib_in[j].astype(f32)

    for j in (5, 6, 7, 4):
        own_half(j)[...] = chip_sum(j).astype(b16)
        begin(remote(own_half(j), y_in.at[j - NZ], y_send.at[j - NZ], y_recv.at[j - NZ], (dp, across)))
    for j in range(NZ):
        pass_across(2, j)

    for j0 in range(0, pairs, 2):
        from_sibling(2, j0)
        for k in range(2):
            base, select, slot_weight = choose(j0 + k)
            both = cot[pl.ds(base * n, NC * n), :]
            scaled = (slot_weight * jnp.dot(select, both, preferred_element_type=f32)).astype(b16)
            back = lax.dot_general(
                scaled, down_ref[...], (((1,), (1,)), ((), ())), preferred_element_type=f32
            )
            at_rows = pl.ds((j0 + k) * height, height)
            coeff[at_rows, :] = (back * factor[at_rows, :]).astype(b16)

    wide = half // 4

    def product(start):
        cols = rows[:, pl.ds(pl.multiple_of(start, 128), wide)]
        return lax.dot_general(
            cols, coeff[...], (((0,), (0,)), ((), ())), preferred_element_type=f32
        )

    for q in range(4):
        some = pl.ds(q * wide, wide)
        x_out[some, :] = product((1 - dp) * half + q * wide).astype(b16)
        begin(remote(x_out.at[some], x_in.at[some], x_send.at[q], x_recv.at[q], other))

    for j in (1, 2, 3, 0):
        total = chip_sum(j)
        landed(y_in.at[j], y_recv.at[j])
        total = total + y_in[j].astype(f32)
        own_half(j)[...] = total.astype(b16)
        if j > 0:
            begin(remote(
                own_half(j), z_in.at[j - 1], z_send.at[j - 1], z_recv.at[j - 1],
                (dp, at(zj(j), y, c)),
            ))
    for q in range(4):
        hvp_ref[pl.ds(q * wide, wide), :] = product(dp * half + q * wide)
    for q in range(4):
        some = pl.ds(q * wide, wide)
        landed(x_in.at[some], x_recv.at[q])
        hvp_ref[some, :] = hvp_ref[some, :] + x_in[some, :].astype(f32)
    for j in range(NZ - 1):
        landed(z_in.at[j], z_recv.at[j])
    out_ref[...] = (
        own_half(0)[...].astype(f32) + z_in[0].astype(f32)
        + z_in[1].astype(f32) + z_in[2].astype(f32)
    ).astype(b16)
    for test, make in sent:
        if test is None:
            make().wait_send()
        else:
            @pl.when(test)
            def _():
                make().wait_send()


def fused(tokens, cotangent, expert_ids, combine, w_gate, w_up, w_down, tangent_gate):
    count = lax.axis_size("expert")
    n, top = expert_ids.shape
    width, hidden = w_gate.shape[1:]
    capacity = n * top * 9 // (8 * count)
    total = count * capacity
    b16, f32 = jnp.bfloat16, jnp.float32
    dma = pltpu.SemaphoreType.DMA
    pairs = NZ * NY
    whole = pl.BlockSpec(memory_space=pltpu.VMEM)
    hvp, out = pl.pallas_call(
        functools.partial(kernel, capacity),
        out_shape=(
            jax.ShapeDtypeStruct((width // 2, hidden), f32),
            jax.ShapeDtypeStruct((n, width), b16),
        ),
        in_specs=[whole] * 7,
        out_specs=(whole, whole),
        scratch_shapes=[
            pltpu.VMEM((count, count, n), f32),
            pltpu.VMEM((count * n, width), b16),
            pltpu.VMEM((count * n, width), b16),
            pltpu.VMEM((total, width), b16),
            pltpu.VMEM((total, hidden), f32),
            pltpu.VMEM((total, hidden), b16),
            pltpu.VMEM((pairs, NC * n, width), b16),
            pltpu.VMEM((pairs, n, width), b16),
            pltpu.VMEM((NZ, n, width), b16),
            pltpu.VMEM((NZ - 1, n, width), b16),
            pltpu.VMEM((width // 2, hidden), b16),
            pltpu.VMEM((width // 2, hidden), b16),
            dma((3, 7 * NZ - 2)), dma((3, count)),
            dma((pairs,)), dma((pairs,)),
            dma((NZ,)), dma((NZ,)),
            dma((NZ - 1,)), dma((NZ - 1,)),
            dma((4,)), dma((4,)),
        ],
        compiler_params=pltpu.CompilerParams(
            collective_id=0, has_side_effects=True, vmem_limit_bytes=63 * 1024 * 1024
        ),
    )(
        weight_table(expert_ids, combine, count), tokens, cotangent,
        w_gate[0], w_up[0], w_down[0], tangent_gate[0],
    )
    return hvp[None], out


def per_device(*arrays):
    if lax.axis_size("expert") == NZ * NY * NC and lax.axis_size("dp") == 2:
        return fused(*arrays)
    return gathered(*arrays)


def solution(mesh):
    rows = P(("dp", "expert"), None)
    owned = P("expert", None, None)
    return jax.shard_map(
        per_device,
        mesh=mesh,
        in_specs=(rows, rows, rows, rows, owned, owned, owned, owned),
        out_specs=(P("expert", "dp", None), rows),
        check_vma=False,
    )
```
